512 devices in a mesh: dp: 4 (over x), mp: 128 (over y, z, core).
Axes of the slice: x: 4, y: 4, z: 16, core: 2. Of those that a mesh axis runs over, the one named last changes fastest.
Arguments:
- inputs: bfloat16 [2048, 128, 128], P('dp', 'mp'), may hold values from -6 to 6
- out_grad: bfloat16 [2048, 128, 128], P('dp', 'mp'), may hold values from -6 to 6
- outer_in: bfloat16 [128, 128, 128], P('mp'), may hold values from -0.5 to 0.5
- inner_up: bfloat16 [128, 128, 512], P('mp'), may hold values from -0.5 to 0.5
- inner_down: bfloat16 [128, 512, 128], P('mp'), may hold values from -0.25 to 0.25
- outer_out: bfloat16 [128, 128, 128], P('mp'), may hold values from -0.5 to 0.5
Outputs:
- mixed: bfloat16 [2048, 128, 128], P('dp', 'mp')
- input_grad: bfloat16 [2048, 128, 128], P('dp', 'mp')
- outer_in_grad: float32 [128, 128, 128], P('mp')
- inner_up_grad: float32 [128, 128, 512], P('mp')
- inner_down_grad: float32 [128, 512, 128], P('mp')
- outer_out_grad: float32 [128, 128, 128], P('mp')
The draws below stay inside these ranges and needn't reach their ends.
All inputs are finite; a program needn't handle non-finite values.
Results may differ from the reference program's by a relative error of at most 0.014.
Values may be sent and summed in bfloat16 or wider, within the bound.
A program may use at most 64 MiB of HBM per device.

```python
import math
import jax
import jax.numpy as jnp
from jax import lax

NB = 128
BS = 128
HB = 512
TOKENS = 2048


def levels(own_key, shape, pieces, least, high):
    def one(position, blocks):
        draws = jax.random.uniform(jax.random.fold_in(jax.random.fold_in(own_key, 6), position), (blocks,), jnp.float32, least / len(pieces), high / len(pieces))
        return jnp.repeat(jnp.exp(draws), shape[position] // blocks).reshape((-1,) + (1,) * (len(shape) - position - 1))

    loudness = one(*pieces[0])
    for cut in pieces[1:]:
        loudness = loudness * one(*cut)
    return loudness


def gaussian(rng, shape, spread, reach, shards=(), kind=jnp.bfloat16):
    level = levels(rng, shape, shards, -0.22, 0.18) if shards else 1.0
    array = jax.random.normal(rng, shape, jnp.float32) * spread * level
    return jnp.minimum(jnp.maximum(array, -reach), reach).astype(kind)


def setup_inputs(seed: int = 0) -> dict:
    arg_keys = jax.random.split(jax.random.key(seed), 7)
    return {
        "inputs": gaussian(arg_keys[0], (TOKENS, NB, BS), 1.0, 6.0, ((0, 4), (1, 128))),
        "out_grad": gaussian(arg_keys[1], (TOKENS, NB, BS), 1.0, 6.0, ((0, 4), (1, 128))),
        "outer_in": gaussian(arg_keys[2], (NB, BS, BS), BS ** -0.5, 0.5, ((0, 128),)),
        "inner_up": gaussian(arg_keys[3], (BS, NB, HB), NB ** -0.5, 0.5, ((0, 128),)),
        "inner_down": gaussian(arg_keys[4], (BS, HB, NB), HB ** -0.5, 0.25, ((0, 128),)),
        "outer_out": gaussian(arg_keys[5], (NB, BS, BS), BS ** -0.5, 0.5, ((0, 128),)),
    }


def gelu_grad(pre_act, grad_hidden):
    _, pull_back = jax.vjp(jax.nn.gelu, pre_act)
    return pull_back(grad_hidden)[0]

def reference(inputs, out_grad, outer_in, inner_up, inner_down, outer_out):
    rows = math.gcd(TOKENS, 256)
    count = TOKENS // rows
    outer_in_wide = outer_in.astype(jnp.float32)
    inner_up_wide = inner_up.astype(jnp.float32)
    inner_down_wide = inner_down.astype(jnp.float32)
    outer_out_wide = outer_out.astype(jnp.float32)

    def one_block(totals, pair):
        block_in, block_grad = pair
        block_in = block_in.astype(jnp.float32)
        block_grad = block_grad.astype(jnp.float32)
        first = jnp.einsum('tbk,bkj->tbj', block_in, outer_in_wide).astype(jnp.bfloat16)
        first_wide = first.astype(jnp.float32)
        pre_act = jnp.einsum('tbj,jbh->tjh', first_wide, inner_up_wide)
        hidden = jax.nn.gelu(pre_act).astype(jnp.bfloat16)
        hidden_wide = hidden.astype(jnp.float32)
        down = jnp.einsum('tjh,jhc->tjc', hidden_wide, inner_down_wide).astype(jnp.bfloat16)
        down_wide = down.astype(jnp.float32)
        mixed_block = jnp.einsum('tjc,cjk->tck', down_wide, outer_out_wide).astype(jnp.bfloat16)
        grad_down = jnp.einsum('tck,cjk->tcj', block_grad, outer_out_wide).astype(jnp.bfloat16)
        grad_down_wide = grad_down.astype(jnp.float32)
        grad_hidden = jnp.einsum('tcj,jhc->tjh', grad_down_wide, inner_down_wide)
        grad_pre = gelu_grad(pre_act, grad_hidden).astype(jnp.bfloat16)
        grad_pre_wide = grad_pre.astype(jnp.float32)
        grad_first = jnp.einsum('tjh,jbh->tjb', grad_pre_wide, inner_up_wide).astype(jnp.bfloat16)
        grad_first_wide = grad_first.astype(jnp.float32)
        grad_block = jnp.einsum('tjb,bkj->tbk', grad_first_wide, outer_in_wide).astype(jnp.bfloat16)
        outer_in_term = jnp.einsum('tbk,tjb->bkj', block_in, grad_first_wide)
        inner_up_term = jnp.einsum('tbj,tjh->jbh', first_wide, grad_pre_wide)
        inner_down_term = jnp.einsum('tjh,tcj->jhc', hidden_wide, grad_down_wide)
        outer_out_term = jnp.einsum('tjc,tck->cjk', down_wide, block_grad)
        new_totals = (totals[0] + outer_in_term, totals[1] + inner_up_term, totals[2] + inner_down_term, totals[3] + outer_out_term)
        return (new_totals, (mixed_block, grad_block))
    start = (jnp.zeros((NB, BS, BS), jnp.float32), jnp.zeros((BS, NB, HB), jnp.float32), jnp.zeros((BS, HB, NB), jnp.float32), jnp.zeros((NB, BS, BS), jnp.float32))
    totals, outputs = lax.scan(one_block, start, (inputs.reshape(count, rows, NB, BS), out_grad.reshape(count, rows, NB, BS)))
    mixed = outputs[0].reshape(TOKENS, NB, BS)
    input_grad = outputs[1].reshape(TOKENS, NB, BS)
    factor = TOKENS ** (-0.5)
    return (mixed, input_grad, totals[0] * factor, totals[1] * factor, totals[2] * factor, totals[3] * factor)
```

```python
import functools

import jax
import jax.numpy as jnp
from jax import lax
from jax.experimental import pallas as pl
from jax.experimental.pallas import tpu as pltpu
from jax.sharding import PartitionSpec as P

BF = jnp.bfloat16
F32 = jnp.float32
MESH = pl.DeviceIdType.MESH
C0 = 0.7978845608028654
C1 = 0.044715


def dot(a, b, ca, cb):
    return lax.dot_general(a, b, (((ca,), (cb,)), ((), ())), preferred_element_type=F32)


def remote(src, dst, send, recv, where):
    return pltpu.make_async_remote_copy(
        src_ref=src, dst_ref=dst, send_sem=send, recv_sem=recv, device_id=where, device_id_type=MESH
    )


def kernel(
    n,
    nd,
    factor,
    x_hbm,
    g_hbm,
    w1_hbm,
    u_hbm,
    d_hbm,
    w2_hbm,
    mixed_ref,
    igrad_ref,
    w1g_ref,
    ug_ref,
    dg_ref,
    w2g_ref,
    x_ref,
    g_ref,
    w1_ref,
    u_ref,
    d_ref,
    w2_ref,
    ut_ref,
    dt_ref,
    s1,
    s2,
    s3,
    s4,
    r1,
    r2,
    r3,
    r4,
    col_ref,
    gcol_ref,
    slope_ref,
    hid_ref,
    gp_ref,
    mid_ref,
    tu,
    td,
    ru,
    rd,
    au,
    ad,
    t_oo,
    r_oo,
    t_oi,
    r_oi,
    load_sem,
    send_sem,
    recv_sem,
    xsend_sem,
    xrecv_sem,
):
    m = lax.axis_index("mp")
    p = lax.axis_index("dp")
    loads = [
        pltpu.make_async_copy(src, dst, load_sem.at[i])
        for i, (src, dst) in enumerate(
            (
                (x_hbm, x_ref),
                (w1_hbm, w1_ref),
                (g_hbm, g_ref),
                (w2_hbm, w2_ref),
                (u_hbm, u_ref),
                (d_hbm, d_ref),
            )
        )
    ]
    for c in loads:
        c.start()

    barrier = pltpu.get_barrier_semaphore()

    @pl.loop(1, n)
    def _(i):
        pl.semaphore_signal(barrier, inc=1, device_id={"mp": (m + i) % n}, device_id_type=MESH)

    @pl.loop(1, nd)
    def _(i):
        pl.semaphore_signal(barrier, inc=1, device_id={"dp": (p + i) % nd}, device_id_type=MESH)

    def send_all(e, src, dst):
        @pl.loop(1, n)
        def _(i):
            to = (m + i) % n
            remote(src.at[to], dst.at[m], send_sem.at[e], recv_sem.at[e], {"mp": to}).start()

        dst[m] = src[m]

    def whole(e, src, dst):
        part = pl.ds(0, n - 1)
        return remote(
            src.at[part], dst.at[part], send_sem.at[e], recv_sem.at[e], {"mp": (m + 1) % n}
        )

    def send_dp(e, src, dst, cut):
        for i in range(1, nd):
            to = (p + i) % nd
            remote(
                src.at[to] if cut else src, dst.at[p], xsend_sem.at[e], xrecv_sem.at[e], {"dp": to}
            ).start()

    def whole_dp(e, dst):
        part = pl.ds(0, nd - 1)
        return remote(
            dst.at[part], dst.at[part], xsend_sem.at[e], xrecv_sem.at[e], {"dp": (p + 1) % nd}
        )

    tokens = x_ref.shape[0]
    blocks = (n, tokens // 128, 128)
    flat = (n, tokens)

    loads[0].wait()
    loads[1].wait()
    s1[...] = dot(w1_ref[...], x_ref[...], 0, 1).astype(BF).reshape(blocks)
    loads[2].wait()
    loads[3].wait()
    s2[...] = dot(w2_ref[...], g_ref[...], 1, 1).astype(BF).reshape(blocks)
    loads[4].wait()
    loads[5].wait()
    ut_ref[...] = u_ref[...].T
    dt_ref[...] = d_ref[...].T

    pl.semaphore_wait(barrier, n - 1 + nd - 1)
    send_all(0, s1, r1)
    send_all(1, s2, r2)

    half = tokens // 2
    whole(0, s1, r1).wait_recv()
    col_ref[...] = r1[...].reshape(flat)
    for q in range(2):
        cols = pl.ds(q * half, half)
        a = dot(ut_ref[...], col_ref[:, cols], 1, 0)
        sq = a * a
        th = jnp.tanh(C0 * (a + C1 * (a * sq)))
        up = 0.5 * (1.0 + th)
        hid = (a * up).astype(BF)
        hid_ref[:, cols] = hid
        slope_ref[:, cols] = up + (0.5 * a) * (1.0 - th * th) * (C0 + (3.0 * C0 * C1) * sq)
        mid_ref[:, cols] = dot(dt_ref[...], hid, 1, 0).astype(BF)
    s3[...] = mid_ref[...].reshape(blocks)
    send_all(2, s3, r3)

    whole(1, s2, r2).wait_recv()
    gcol_ref[...] = r2[...].reshape(flat)
    for q in range(2):
        cols = pl.ds(q * half, half)
        gh = dot(d_ref[...], gcol_ref[:, cols], 1, 0)
        gp = (gh * slope_ref[:, cols]).astype(BF)
        gp_ref[:, cols] = gp
        mid_ref[:, cols] = dot(u_ref[...], gp, 1, 0).astype(BF)
    s4[...] = mid_ref[...].reshape(blocks)
    send_all(3, s4, r4)

    tu[...] = dot(col_ref[...], gp_ref[...], 1, 1).astype(BF).reshape(tu.shape)
    td[...] = dot(hid_ref[...], gcol_ref[...], 1, 1).astype(BF).reshape(td.shape)
    send_dp(0, tu, ru, True)
    send_dp(1, td, rd, True)
    ru[p] = tu[p]
    rd[p] = td[p]

    whole(2, s3, r3).wait_recv()
    rows = r3[...].reshape(flat)
    t_oo[...] = dot(rows, g_ref[...], 1, 0).astype(BF)
    send_dp(2, t_oo, r_oo, False)
    r_oo[p] = t_oo[...]
    mixed_ref[...] = dot(rows, w2_ref[...], 0, 0).astype(BF)

    def added(r):
        total = r[0].astype(F32)
        for i in range(1, nd):
            total += r[i].astype(F32)
        return total

    whole_dp(0, ru).wait()
    au[p] = added(ru).astype(BF)
    whole_dp(1, rd).wait()
    ad[p] = added(rd).astype(BF)
    send_dp(3, au.at[p], au, False)
    send_dp(4, ad.at[p], ad, False)

    whole(3, s4, r4).wait_recv()
    rows = r4[...].reshape(flat)
    t_oi[...] = dot(x_ref[...], rows, 0, 1).astype(BF)
    send_dp(5, t_oi, r_oi, False)
    r_oi[p] = t_oi[...]
    igrad_ref[...] = dot(rows, w1_ref[...], 0, 1).astype(BF)

    whole_dp(3, au).wait()
    whole_dp(4, ad).wait()
    ug_ref[...] = au[...].astype(F32).reshape(ug_ref.shape) * factor
    dg_ref[...] = ad[...].astype(F32).reshape(dg_ref.shape) * factor
    whole_dp(2, r_oo).wait()
    w2g_ref[...] = added(r_oo) * factor
    whole(0, s1, r1).wait_send()
    whole(1, s2, r2).wait_send()
    whole(2, s3, r3).wait_send()
    whole(3, s4, r4).wait_send()
    whole_dp(5, r_oi).wait()
    w1g_ref[...] = added(r_oi) * factor


def local(n, nd, inputs, out_grad, outer_in, inner_up, inner_down, outer_out):
    t, _, k = inputs.shape
    h = inner_up.shape[2]
    x, g = inputs.reshape(t, k), out_grad.reshape(t, k)
    w1, u, d, w2 = outer_in[0], inner_up[0], inner_down[0], outer_out[0]
    shape = jax.ShapeDtypeStruct
    vm = pltpu.VMEM
    lanes = t // 128
    blocks = vm((n, lanes, 128), BF)
    outs = pl.pallas_call(
        functools.partial(kernel, n, nd, float(t * nd) ** -0.5),
        out_shape=(
            shape((t, k), BF),
            shape((t, k), BF),
            shape((k, n), F32),
            shape((n, h), F32),
            shape((h, n), F32),
            shape((n, k), F32),
        ),
        in_specs=[pl.BlockSpec(memory_space=pl.ANY)] * 6,
        out_specs=[pl.BlockSpec(memory_space=pltpu.VMEM)] * 6,
        scratch_shapes=[
            vm((t, k), BF),
            vm((t, k), BF),
            vm((k, n), BF),
            vm((n, h), BF),
            vm((h, n), BF),
            vm((n, k), BF),
            vm((h, n), BF),
            vm((n, h), BF),
        ]
        + [blocks] * 8
        + [
            vm((n, t), BF),
            vm((n, t), BF),
            vm((h, t), F32),
            vm((h, t), BF),
            vm((h, t), BF),
            vm((n, t), BF),
            vm((nd, n // nd, h), BF),
            vm((nd, h // nd, n), BF),
            vm((nd, n // nd, h), BF),
            vm((nd, h // nd, n), BF),
            vm((nd, n // nd, h), BF),
            vm((nd, h // nd, n), BF),
            vm((n, k), BF),
            vm((nd, n, k), BF),
            vm((k, n), BF),
            vm((nd, k, n), BF),
            pltpu.SemaphoreType.DMA((6,)),
            pltpu.SemaphoreType.DMA((4,)),
            pltpu.SemaphoreType.DMA((4,)),
            pltpu.SemaphoreType.DMA((6,)),
            pltpu.SemaphoreType.DMA((6,)),
        ],
        compiler_params=pltpu.CompilerParams(
            collective_id=0, has_side_effects=True, vmem_limit_bytes=32 * 1024 * 1024
        ),
    )(x, g, w1, u, d, w2)
    mixed, igrad, w1g, ug, dg, w2g = outs
    return (
        mixed.reshape(t, 1, k),
        igrad.reshape(t, 1, k),
        w1g[None],
        ug[None],
        dg[None],
        w2g[None],
    )


def solution(mesh):
    n, nd = mesh.shape["mp"], mesh.shape["dp"]
    specs = (
        P("dp", "mp", None),
        P("dp", "mp", None),
        P("mp", None, None),
        P("mp", None, None),
        P("mp", None, None),
        P("mp", None, None),
    )
    return jax.shard_map(
        functools.partial(local, n, nd), mesh=mesh, in_specs=specs, out_specs=specs, check_vma=False
    )
```

```python
import functools

import jax
import jax.numpy as jnp
from jax import lax
from jax.experimental import pallas as pl
from jax.experimental.pallas import tpu as pltpu
from jax.sharding import PartitionSpec as P

BF = jnp.bfloat16
F32 = jnp.float32
MESH = pl.DeviceIdType.MESH
DEPTH = 16
C0 = 0.7978845608028654
C1 = 0.044715


def dot(a, b, ca, cb):
    return lax.dot_general(a, b, (((ca,), (cb,)), ((), ())), preferred_element_type=F32)


def remote(src, dst, send, recv, where):
    return pltpu.make_async_remote_copy(
        src_ref=src, dst_ref=dst, send_sem=send, recv_sem=recv, device_id=where, device_id_type=MESH
    )


def kernel(
    n,
    nd,
    factor,
    x_hbm,
    g_hbm,
    w1_hbm,
    u_hbm,
    d_hbm,
    w2_hbm,
    mixed_ref,
    igrad_ref,
    w1g_ref,
    ug_ref,
    dg_ref,
    w2g_ref,
    x_ref,
    g_ref,
    w1_ref,
    u_ref,
    d_ref,
    w2_ref,
    ut_ref,
    dt_ref,
    w1t_ref,
    s1,
    s2,
    s3,
    s4,
    r1,
    r2,
    r3,
    r4,
    col_ref,
    gcol_ref,
    slope_ref,
    hid_ref,
    gp_ref,
    mid_ref,
    tu,
    td,
    ru,
    rd,
    au,
    ad,
    t_oo,
    r_oo,
    t_oi,
    r_oi,
    load_sem,
    send_sem,
    recv_sem,
    xsend_sem,
    xrecv_sem,
    out_sem,
    mixed_v,
    igrad_v,
    w1g_v,
    ug_v,
    dg_v,
    w2g_v,
):
    m = lax.axis_index("mp")
    p = lax.axis_index("dp")
    loads = [
        pltpu.make_async_copy(src, dst, load_sem.at[i])
        for i, (src, dst) in enumerate(
            (
                (x_hbm, x_ref),
                (w1_hbm, w1_ref),
                (g_hbm, g_ref),
                (w2_hbm, w2_ref),
                (u_hbm, u_ref),
                (d_hbm, d_ref),
            )
        )
    ]
    for c in loads:
        c.start()

    barrier = pltpu.get_barrier_semaphore()

    plane = n // DEPTH
    z = (m // 2) % DEPTH
    yc = (m // (2 * DEPTH)) * 2 + m % 2
    bases = []
    for k in range(plane - 1, -1, -1):
        t = (yc + k) % plane
        bases.append((t // 2) * (2 * DEPTH) + t % 2)

    def partners(act):
        @pl.loop(0, DEPTH - 1)
        def _(i):
            far = (DEPTH - i) // 2
            zt = (z + DEPTH + far * (1 - 2 * (i % 2))) % DEPTH
            for base in bases:
                act(base + 2 * zt)

        for base in bases[:-1]:
            act(base + 2 * z)

    def greet(to):
        pl.semaphore_signal(barrier, inc=1, device_id={"mp": to}, device_id_type=MESH)

    partners(greet)
    for i in range(1, nd):
        pl.semaphore_signal(barrier, inc=1, device_id={"dp": (p + i) % nd}, device_id_type=MESH)

    def send_all(e, src, dst):
        def act(to):
            remote(src.at[to], dst.at[m], send_sem.at[e], recv_sem.at[e], {"mp": to}).start()

        partners(act)
        dst[m] = src[m]

    def whole(e, src, dst):
        part = pl.ds(0, n - 1)
        return remote(
            src.at[part], dst.at[part], send_sem.at[e], recv_sem.at[e], {"mp": (m + 1) % n}
        )

    def send_dp(e, src, dst, cut):
        for i in range(1, nd):
            to = (p + i) % nd
            remote(
                src.at[to] if cut else src, dst.at[p], xsend_sem.at[e], xrecv_sem.at[e], {"dp": to}
            ).start()

    def whole_dp(e, dst):
        part = pl.ds(0, nd - 1)
        return remote(
            dst.at[part], dst.at[part], xsend_sem.at[e], xrecv_sem.at[e], {"dp": (p + 1) % nd}
        )

    outs = []

    def store_out(i, src, dst):
        c = pltpu.make_async_copy(src, dst, out_sem.at[i])
        c.start()
        outs.append(c)

    tokens = x_ref.shape[0]
    blocks = (n, tokens // 128, 128)
    flat = (n, tokens)

    loads[0].wait()
    loads[1].wait()
    s1[...] = dot(w1_ref[...], x_ref[...], 0, 1).astype(BF).reshape(blocks)
    pl.semaphore_wait(barrier, n - 1 + nd - 1)
    send_all(0, s1, r1)
    loads[2].wait()
    loads[3].wait()
    s2[...] = dot(w2_ref[...], g_ref[...], 1, 1).astype(BF).reshape(blocks)
    send_all(1, s2, r2)
    loads[4].wait()
    loads[5].wait()
    ut_ref[...] = u_ref[...].T
    dt_ref[...] = d_ref[...].T
    w1t_ref[...] = w1_ref[...].T

    half = tokens // 2
    whole(0, s1, r1).wait_recv()
    col_ref[...] = r1[...].reshape(flat)
    for q in range(2):
        cols = pl.ds(q * half, half)
        a = dot(ut_ref[...], col_ref[:, cols], 1, 0)
        sq = a * a
        th = jnp.tanh(C0 * (a + C1 * (a * sq)))
        up = 0.5 * (1.0 + th)
        hid = (a * up).astype(BF)
        hid_ref[:, cols] = hid
        slope_ref[:, cols] = up + (0.5 * a) * (1.0 - th * th) * (C0 + (3.0 * C0 * C1) * sq)
        mid_ref[:, cols] = dot(dt_ref[...], hid, 1, 0).astype(BF)
    s3[...] = mid_ref[...].reshape(blocks)
    send_all(2, s3, r3)

    whole(1, s2, r2).wait_recv()
    gcol_ref[...] = r2[...].reshape(flat)
    for q in range(2):
        cols = pl.ds(q * half, half)
        gh = dot(d_ref[...], gcol_ref[:, cols], 1, 0)
        gp = (gh * slope_ref[:, cols]).astype(BF)
        gp_ref[:, cols] = gp
        mid_ref[:, cols] = dot(u_ref[...], gp, 1, 0).astype(BF)
    s4[...] = mid_ref[...].reshape(blocks)
    send_all(3, s4, r4)

    tu[...] = dot(col_ref[...], gp_ref[...], 1, 1).astype(BF).reshape(tu.shape)
    td[...] = dot(hid_ref[...], gcol_ref[...], 1, 1).astype(BF).reshape(td.shape)
    send_dp(0, tu, ru, True)
    send_dp(1, td, rd, True)
    ru[p] = tu[p]
    rd[p] = td[p]

    whole(2, s3, r3).wait_recv()
    rows = r3[...].reshape(flat)
    t_oo[...] = dot(rows, g_ref[...], 1, 0).astype(BF)
    send_dp(2, t_oo, r_oo, False)
    r_oo[p] = t_oo[...]
    mixed_v[...] = dot(rows, w2_ref[...], 0, 0).astype(BF)

    store_out(0, mixed_v, mixed_ref)

    def added(r):
        total = r[0].astype(F32)
        for i in range(1, nd):
            total += r[i].astype(F32)
        return total

    whole_dp(0, ru).wait()
    au[p] = added(ru).astype(BF)
    whole_dp(1, rd).wait()
    ad[p] = added(rd).astype(BF)
    send_dp(3, au.at[p], au, False)
    send_dp(4, ad.at[p], ad, False)

    whole_dp(2, r_oo).wait()
    w2g_v[...] = added(r_oo) * factor
    store_out(5, w2g_v, w2g_ref)
    whole_dp(3, au).wait()
    ug_v[...] = au[...].astype(F32).reshape(ug_ref.shape) * factor
    store_out(3, ug_v, ug_ref)
    whole_dp(4, ad).wait()
    dg_v[...] = ad[...].astype(F32).reshape(dg_ref.shape) * factor
    store_out(4, dg_v, dg_ref)
    whole(0, s1, r1).wait_send()
    whole(1, s2, r2).wait_send()
    whole(2, s3, r3).wait_send()

    whole(3, s4, r4).wait_recv()
    rows = r4[...].reshape(flat)
    t_oi[...] = dot(rows, x_ref[...], 1, 0).astype(BF)
    send_dp(5, t_oi, r_oi, False)
    r_oi[p] = t_oi[...]
    igrad_v[...] = dot(rows, w1t_ref[...], 0, 0).astype(BF)
    store_out(1, igrad_v, igrad_ref)
    whole(3, s4, r4).wait_send()
    whole_dp(5, r_oi).wait()
    w1g_v[...] = added(r_oi).T * factor
    store_out(2, w1g_v, w1g_ref)
    for c in outs:
        c.wait()


def store(*refs):
    src, dst, mid, sem = refs[:6], refs[6:12], refs[12:18], refs[18]
    into = [pltpu.make_async_copy(src[i], mid[i], sem.at[i]) for i in range(6)]
    out = [pltpu.make_async_copy(mid[i], dst[i], sem.at[6 + i]) for i in range(6)]
    for c in into:
        c.start()
    for i in range(6):
        into[i].wait()
        out[i].start()
    for c in out:
        c.wait()


def local(n, nd, inputs, out_grad, outer_in, inner_up, inner_down, outer_out):
    t, _, k = inputs.shape
    h = inner_up.shape[2]
    x, g = inputs.reshape(t, k), out_grad.reshape(t, k)
    w1, u, d, w2 = outer_in[0], inner_up[0], inner_down[0], outer_out[0]
    shape = jax.ShapeDtypeStruct
    vm = pltpu.VMEM
    lanes = t // 128
    blocks = vm((n, lanes, 128), BF)
    outs = pl.pallas_call(
        functools.partial(kernel, n, nd, float(t * nd) ** -0.5),
        out_shape=(
            shape((t, k), BF),
            shape((t, k), BF),
            shape((k, n), F32),
            shape((n, h), F32),
            shape((h, n), F32),
            shape((n, k), F32),
        ),
        in_specs=[pl.BlockSpec(memory_space=pl.ANY)] * 6,
        out_specs=[pl.BlockSpec(memory_space=pl.ANY)] * 6,
        scratch_shapes=[
            vm((t, k), BF),
            vm((t, k), BF),
            vm((k, n), BF),
            vm((n, h), BF),
            vm((h, n), BF),
            vm((n, k), BF),
            vm((h, n), BF),
            vm((n, h), BF),
            vm((n, k), BF),
        ]
        + [blocks] * 8
        + [
            vm((n, t), BF),
            vm((n, t), BF),
            vm((h, t), F32),
            vm((h, t), BF),
            vm((h, t), BF),
            vm((n, t), BF),
            vm((nd, n // nd, h), BF),
            vm((nd, h // nd, n), BF),
            vm((nd, n // nd, h), BF),
            vm((nd, h // nd, n), BF),
            vm((nd, n // nd, h), BF),
            vm((nd, h // nd, n), BF),
            vm((n, k), BF),
            vm((nd, n, k), BF),
            vm((n, k), BF),
            vm((nd, n, k), BF),
            pltpu.SemaphoreType.DMA((6,)),
            pltpu.SemaphoreType.DMA((4,)),
            pltpu.SemaphoreType.DMA((4,)),
            pltpu.SemaphoreType.DMA((6,)),
            pltpu.SemaphoreType.DMA((6,)),
            pltpu.SemaphoreType.DMA((6,)),
            vm((t, k), BF),
            vm((t, k), BF),
            vm((k, n), F32),
            vm((n, h), F32),
            vm((h, n), F32),
            vm((n, k), F32),
        ],
        compiler_params=pltpu.CompilerParams(
            collective_id=0, has_side_effects=True, vmem_limit_bytes=62 * 1024 * 1024
        ),
    )(x, g, w1, u, d, w2)
    outs = pl.pallas_call(
        store,
        out_shape=tuple(shape(o.shape, o.dtype) for o in outs),
        in_specs=[pl.BlockSpec(memory_space=pl.ANY)] * 6,
        out_specs=[pl.BlockSpec(memory_space=pl.ANY)] * 6,
        scratch_shapes=[vm(o.shape, o.dtype) for o in outs] + [pltpu.SemaphoreType.DMA((12,))],
        compiler_params=pltpu.CompilerParams(vmem_limit_bytes=62 * 1024 * 1024),
    )(*outs)
    mixed, igrad, w1g, ug, dg, w2g = outs
    return (
        mixed.reshape(t, 1, k),
        igrad.reshape(t, 1, k),
        w1g[None],
        ug[None],
        dg[None],
        w2g[None],
    )


def solution(mesh):
    n, nd = mesh.shape["mp"], mesh.shape["dp"]
    specs = (
        P("dp", "mp", None),
        P("dp", "mp", None),
        P("mp", None, None),
        P("mp", None, None),
        P("mp", None, None),
        P("mp", None, None),
    )
    return jax.shard_map(
        functools.partial(local, n, nd), mesh=mesh, in_specs=specs, out_specs=specs, check_vma=False
    )
```

```python
import functools

import jax
import jax.numpy as jnp
from jax import lax
from jax.experimental import pallas as pl
from jax.experimental.pallas import tpu as pltpu
from jax.sharding import PartitionSpec as P

BF = jnp.bfloat16
F32 = jnp.float32
MESH = pl.DeviceIdType.MESH
DEPTH = 16
C0 = 0.7978845608028654
C1 = 0.044715


def dot(a, b, ca, cb):
    return lax.dot_general(a, b, (((ca,), (cb,)), ((), ())), preferred_element_type=F32)


def remote(src, dst, send, recv, where):
    return pltpu.make_async_remote_copy(
        src_ref=src, dst_ref=dst, send_sem=send, recv_sem=recv, device_id=where, device_id_type=MESH
    )


def kernel(
    n,
    nd,
    factor,
    x_hbm,
    g_hbm,
    w1_hbm,
    u_hbm,
    d_hbm,
    w2_hbm,
    mixed_ref,
    igrad_ref,
    w1g_ref,
    ug_ref,
    dg_ref,
    w2g_ref,
    x_ref,
    g_ref,
    w1_ref,
    u_ref,
    d_ref,
    w2_ref,
    ut_ref,
    dt_ref,
    w1t_ref,
    s1,
    s2,
    s3,
    s4,
    r1,
    r2,
    r3,
    r4,
    col_ref,
    gcol_ref,
    slope_ref,
    hid_ref,
    gp_ref,
    mid_ref,
    tu,
    td,
    ru,
    rd,
    au,
    ad,
    t_oo,
    r_oo,
    t_oi,
    r_oi,
    load_sem,
    send_sem,
    recv_sem,
    xsend_sem,
    xrecv_sem,
    out_sem,
    mixed_v,
    igrad_v,
    w1g_v,
    ug_v,
    dg_v,
    w2g_v,
):
    m = lax.axis_index("mp")
    p = lax.axis_index("dp")
    loads = [
        pltpu.make_async_copy(src, dst, load_sem.at[i])
        for i, (src, dst) in enumerate(
            (
                (x_hbm, x_ref),
                (w1_hbm, w1_ref),
                (g_hbm, g_ref),
                (w2_hbm, w2_ref),
                (u_hbm, u_ref),
                (d_hbm, d_ref),
            )
        )
    ]
    for c in loads:
        c.start()

    barrier = pltpu.get_barrier_semaphore()

    plane = n // DEPTH
    z = (m // 2) % DEPTH
    yc = (m // (2 * DEPTH)) * 2 + m % 2
    bases = []
    for k in range(plane - 1, -1, -1):
        t = (yc + k) % plane
        bases.append((t // 2) * (2 * DEPTH) + t % 2)

    def partners(act, lo=0, hi=DEPTH - 1):
        @pl.loop(lo, hi)
        def _(i):
            far = (DEPTH - i) // 2
            zt = (z + DEPTH + far * (1 - 2 * (i % 2))) % DEPTH
            for base in bases:
                act(base + 2 * zt)

        if hi == DEPTH - 1:
            for base in bases[:-1]:
                act(base + 2 * z)

    def greet(to):
        pl.semaphore_signal(barrier, inc=1, device_id={"mp": to}, device_id_type=MESH)

    partners(greet)
    for i in range(1, nd):
        pl.semaphore_signal(barrier, inc=1, device_id={"dp": (p + i) % nd}, device_id_type=MESH)

    def send_all(e, src, dst, lo=0, hi=DEPTH - 1):
        def act(to):
            remote(src.at[to], dst.at[m], send_sem.at[e], recv_sem.at[e], {"mp": to}).start()

        partners(act, lo, hi)
        if lo == 0:
            dst[m] = src[m]

    def whole(e, src, dst):
        part = pl.ds(0, n - 1)
        return remote(
            src.at[part], dst.at[part], send_sem.at[e], recv_sem.at[e], {"mp": (m + 1) % n}
        )

    def send_dp(e, src, dst, cut):
        for i in range(1, nd):
            to = (p + i) % nd
            remote(
                src.at[to] if cut else src, dst.at[p], xsend_sem.at[e], xrecv_sem.at[e], {"dp": to}
            ).start()

    def whole_dp(e, dst):
        part = pl.ds(0, nd - 1)
        return remote(
            dst.at[part], dst.at[part], xsend_sem.at[e], xrecv_sem.at[e], {"dp": (p + 1) % nd}
        )

    outs = []

    def store_out(i, src, dst):
        c = pltpu.make_async_copy(src, dst, out_sem.at[i])
        c.start()
        outs.append(c)

    def added(r):
        total = r[0].astype(F32)
        for i in range(1, nd):
            total += r[i].astype(F32)
        return total

    tokens = x_ref.shape[0]
    blocks = (n, tokens // 128, 128)
    flat = (n, tokens)

    loads[0].wait()
    loads[1].wait()
    s1[...] = dot(w1_ref[...], x_ref[...], 0, 1).astype(BF).reshape(blocks)
    pl.semaphore_wait(barrier, n - 1 + nd - 1)
    send_all(0, s1, r1)
    loads[2].wait()
    loads[3].wait()
    s2[...] = dot(w2_ref[...], g_ref[...], 1, 1).astype(BF).reshape(blocks)
    send_all(1, s2, r2)
    loads[4].wait()
    loads[5].wait()
    ut_ref[...] = u_ref[...].T
    dt_ref[...] = d_ref[...].T
    w1t_ref[...] = w1_ref[...].T

    half = tokens // 2
    whole(0, s1, r1).wait_recv()
    col_ref[...] = r1[...].reshape(flat)
    for q in range(2):
        cols = pl.ds(q * half, half)
        a = dot(ut_ref[...], col_ref[:, cols], 1, 0)
        sq = a * a
        th = jnp.tanh(C0 * (a + C1 * (a * sq)))
        up = 0.5 * (1.0 + th)
        hid = (a * up).astype(BF)
        hid_ref[:, cols] = hid
        slope_ref[:, cols] = up + (0.5 * a) * (1.0 - th * th) * (C0 + (3.0 * C0 * C1) * sq)
        mid_ref[:, cols] = dot(dt_ref[...], hid, 1, 0).astype(BF)
    s3[...] = mid_ref[...].reshape(blocks)
    send_all(2, s3, r3)

    whole(1, s2, r2).wait_recv()
    gcol_ref[...] = r2[...].reshape(flat)
    td[...] = dot(hid_ref[...], gcol_ref[...], 1, 1).astype(BF).reshape(td.shape)
    send_dp(1, td, rd, True)
    for q in range(2):
        cols = pl.ds(q * half, half)
        gh = dot(d_ref[...], gcol_ref[:, cols], 1, 0)
        gp = (gh * slope_ref[:, cols]).astype(BF)
        gp_ref[:, cols] = gp
        mid_ref[:, cols] = dot(u_ref[...], gp, 1, 0).astype(BF)
    tu[...] = dot(col_ref[...], gp_ref[...], 1, 1).astype(BF).reshape(tu.shape)
    send_dp(0, tu, ru, True)
    s4[...] = mid_ref[...].reshape(blocks)
    send_all(3, s4, r4, 0, 8)
    ru[p] = tu[p]
    rd[p] = td[p]
    whole_dp(0, ru).wait()
    au[p] = added(ru).astype(BF)
    whole_dp(1, rd).wait()
    ad[p] = added(rd).astype(BF)
    send_dp(3, au.at[p], au, False)
    send_dp(4, ad.at[p], ad, False)
    send_all(3, s4, r4, 8)


    whole(2, s3, r3).wait_recv()
    rows = r3[...].reshape(flat)
    t_oo[...] = dot(rows, g_ref[...], 1, 0).astype(BF)
    send_dp(2, t_oo, r_oo, False)
    r_oo[p] = t_oo[...]
    mixed_v[...] = dot(rows, w2_ref[...], 0, 0).astype(BF)

    store_out(0, mixed_v, mixed_ref)


    whole_dp(2, r_oo).wait()
    w2g_v[...] = added(r_oo) * factor
    store_out(5, w2g_v, w2g_ref)
    whole_dp(3, au).wait()
    ug_v[...] = au[...].astype(F32).reshape(ug_ref.shape) * factor
    store_out(3, ug_v, ug_ref)
    whole_dp(4, ad).wait()
    dg_v[...] = ad[...].astype(F32).reshape(dg_ref.shape) * factor
    store_out(4, dg_v, dg_ref)
    whole(0, s1, r1).wait_send()
    whole(1, s2, r2).wait_send()
    whole(2, s3, r3).wait_send()

    whole(3, s4, r4).wait_recv()
    rows = r4[...].reshape(flat)
    t_oi[...] = dot(rows, x_ref[...], 1, 0).astype(BF)
    send_dp(5, t_oi, r_oi, False)
    r_oi[p] = t_oi[...]
    igrad_v[...] = dot(rows, w1t_ref[...], 0, 0).astype(BF)
    store_out(1, igrad_v, igrad_ref)
    whole(3, s4, r4).wait_send()
    whole_dp(5, r_oi).wait()
    w1g_v[...] = added(r_oi).T * factor
    store_out(2, w1g_v, w1g_ref)
    for c in outs:
        c.wait()


def store(*refs):
    src, dst, mid, sem = refs[:6], refs[6:12], refs[12:18], refs[18]
    into = [pltpu.make_async_copy(src[i], mid[i], sem.at[i]) for i in range(6)]
    out = [pltpu.make_async_copy(mid[i], dst[i], sem.at[6 + i]) for i in range(6)]
    for c in into:
        c.start()
    for i in range(6):
        into[i].wait()
        out[i].start()
    for c in out:
        c.wait()


def local(n, nd, inputs, out_grad, outer_in, inner_up, inner_down, outer_out):
    t, _, k = inputs.shape
    h = inner_up.shape[2]
    x, g = inputs.reshape(t, k), out_grad.reshape(t, k)
    w1, u, d, w2 = outer_in[0], inner_up[0], inner_down[0], outer_out[0]
    shape = jax.ShapeDtypeStruct
    vm = pltpu.VMEM
    lanes = t // 128
    blocks = vm((n, lanes, 128), BF)
    outs = pl.pallas_call(
        functools.partial(kernel, n, nd, float(t * nd) ** -0.5),
        out_shape=(
            shape((t, k), BF),
            shape((t, k), BF),
            shape((k, n), F32),
            shape((n, h), F32),
            shape((h, n), F32),
            shape((n, k), F32),
        ),
        in_specs=[pl.BlockSpec(memory_space=pl.ANY)] * 6,
        out_specs=[pl.BlockSpec(memory_space=pl.ANY)] * 6,
        scratch_shapes=[
            vm((t, k), BF),
            vm((t, k), BF),
            vm((k, n), BF),
            vm((n, h), BF),
            vm((h, n), BF),
            vm((n, k), BF),
            vm((h, n), BF),
            vm((n, h), BF),
            vm((n, k), BF),
        ]
        + [blocks] * 8
        + [
            vm((n, t), BF),
            vm((n, t), BF),
            vm((h, t), F32),
            vm((h, t), BF),
            vm((h, t), BF),
            vm((n, t), BF),
            vm((nd, n // nd, h), BF),
            vm((nd, h // nd, n), BF),
            vm((nd, n // nd, h), BF),
            vm((nd, h // nd, n), BF),
            vm((nd, n // nd, h), BF),
            vm((nd, h // nd, n), BF),
            vm((n, k), BF),
            vm((nd, n, k), BF),
            vm((n, k), BF),
            vm((nd, n, k), BF),
            pltpu.SemaphoreType.DMA((6,)),
            pltpu.SemaphoreType.DMA((4,)),
            pltpu.SemaphoreType.DMA((4,)),
            pltpu.SemaphoreType.DMA((6,)),
            pltpu.SemaphoreType.DMA((6,)),
            pltpu.SemaphoreType.DMA((6,)),
            vm((t, k), BF),
            vm((t, k), BF),
            vm((k, n), F32),
            vm((n, h), F32),
            vm((h, n), F32),
            vm((n, k), F32),
        ],
        compiler_params=pltpu.CompilerParams(
            collective_id=0, has_side_effects=True, vmem_limit_bytes=62 * 1024 * 1024
        ),
    )(x, g, w1, u, d, w2)
    outs = pl.pallas_call(
        store,
        out_shape=tuple(shape(o.shape, o.dtype) for o in outs),
        in_specs=[pl.BlockSpec(memory_space=pl.ANY)] * 6,
        out_specs=[pl.BlockSpec(memory_space=pl.ANY)] * 6,
        scratch_shapes=[vm(o.shape, o.dtype) for o in outs] + [pltpu.SemaphoreType.DMA((12,))],
        compiler_params=pltpu.CompilerParams(vmem_limit_bytes=62 * 1024 * 1024),
    )(*outs)
    mixed, igrad, w1g, ug, dg, w2g = outs
    return (
        mixed.reshape(t, 1, k),
        igrad.reshape(t, 1, k),
        w1g[None],
        ug[None],
        dg[None],
        w2g[None],
    )


def solution(mesh):
    n, nd = mesh.shape["mp"], mesh.shape["dp"]
    specs = (
        P("dp", "mp", None),
        P("dp", "mp", None),
        P("mp", None, None),
        P("mp", None, None),
        P("mp", None, None),
        P("mp", None, None),
    )
    return jax.shard_map(
        functools.partial(local, n, nd), mesh=mesh, in_specs=specs, out_specs=specs, check_vma=False
    )
```

```python
import functools

import jax
import jax.numpy as jnp
from jax import lax
from jax.experimental import pallas as pl
from jax.experimental.pallas import tpu as pltpu
from jax.sharding import PartitionSpec as P

BF = jnp.bfloat16
F32 = jnp.float32
MESH = pl.DeviceIdType.MESH
DEPTH = 16
FAR = 10
C0 = 0.7978845608028654
C1 = 0.044715


def dot(a, b, ca, cb):
    return lax.dot_general(a, b, (((ca,), (cb,)), ((), ())), preferred_element_type=F32)


def remote(src, dst, send, recv, where):
    return pltpu.make_async_remote_copy(
        src_ref=src, dst_ref=dst, send_sem=send, recv_sem=recv, device_id=where, device_id_type=MESH
    )


def kernel(
    n,
    nd,
    factor,
    x_hbm,
    g_hbm,
    w1_hbm,
    u_hbm,
    d_hbm,
    w2_hbm,
    mixed_ref,
    igrad_ref,
    w1g_ref,
    ug_ref,
    dg_ref,
    w2g_ref,
    x_ref,
    g_ref,
    w1_ref,
    u_ref,
    d_ref,
    w2_ref,
    ut_ref,
    dt_ref,
    w1t_ref,
    rel_ref,
    acc_ref,
    s1,
    s2,
    s3,
    s4,
    r1,
    r2,
    r3,
    r4,
    col_ref,
    gcol_ref,
    slope_ref,
    th_ref,
    hid_ref,
    gp_ref,
    mid_ref,
    tu,
    td,
    ru,
    rd,
    au,
    ad,
    t_oo,
    r_oo,
    t_oi,
    r_oi,
    t_oj,
    r_oj,
    load_sem,
    send_sem,
    recv_sem,
    xsend_sem,
    xrecv_sem,
    out_sem,
    mixed_v,
    igrad_v,
    w1g_v,
    ug_v,
    dg_v,
    w2g_v,
):
    m = lax.axis_index("mp")
    p = lax.axis_index("dp")
    loads = [
        pltpu.make_async_copy(src, dst, load_sem.at[i])
        for i, (src, dst) in enumerate(
            (
                (x_hbm, x_ref),
                (w1_hbm, w1_ref),
                (g_hbm, g_ref),
                (w2_hbm, w2_ref),
                (u_hbm, u_ref),
                (d_hbm, d_ref),
            )
        )
    ]
    for c in loads:
        c.start()

    barrier = pltpu.get_barrier_semaphore()

    plane = n // DEPTH
    z = (m // 2) % DEPTH
    yc = (m // (2 * DEPTH)) * 2 + m % 2
    bases = []
    for k in range(plane - 1, -1, -1):
        t = (yc + k) % plane
        bases.append((t // 2) * (2 * DEPTH) + t % 2)

    def partners(act):
        @pl.loop(0, DEPTH - 1)
        def _(i):
            far = (DEPTH - i) // 2
            zt = (z + DEPTH + far * (1 - 2 * (i % 2))) % DEPTH
            for base in bases:
                act(base + 2 * zt)

        for base in bases[:-1]:
            act(base + 2 * z)

    steps = [(z + DEPTH + ((DEPTH - q) // 2) * (1 - 2 * (q % 2))) % DEPTH for q in range(DEPTH - 1)]
    slot_z = steps[1 : FAR + 1] + steps[:1] + steps[FAR + 1 :] + [z]

    def greet(to):
        pl.semaphore_signal(barrier, inc=1, device_id={"mp": to}, device_id_type=MESH)

    partners(greet)
    for i in range(1, nd):
        pl.semaphore_signal(barrier, inc=1, device_id={"dp": (p + i) % nd}, device_id_type=MESH)

    def send_all(e, src, dst):
        def act(to):
            remote(src.at[to], dst.at[m], send_sem.at[e], recv_sem.at[e], {"mp": to}).start()

        partners(act)
        dst[m] = src[m]

    def send_last(lo, hi):
        @pl.loop(lo, hi)
        def _(i):
            far = (DEPTH - i) // 2
            zt = (z + DEPTH + far * (1 - 2 * (i % 2))) % DEPTH
            slot = i + 2 * (i % 2) - (2 if hi <= FAR + 1 else 1)
            for base in bases:
                put_last(base + 2 * zt, slot, 3 if hi <= FAR + 1 else 4)

    def put_last(to, slot, e):
        remote(
            s4.at[to], r4.at[slot * plane + yc], send_sem.at[3], recv_sem.at[e], {"mp": to}
        ).start()

    def reorder(dst, src, lo, hi, into):
        for j in range(lo, hi):
            for y in range(plane // 2):
                here = pl.ds(j * plane + 2 * y, 2)
                there = pl.ds(y * (2 * DEPTH) + 2 * slot_z[j], 2)
                if into:
                    dst[here, :] = src[there, :]
                else:
                    dst[there, :] = src[here, :]

    def whole(e, src, dst):
        part = pl.ds(0, n - 1)
        return remote(
            src.at[part], dst.at[part], send_sem.at[e], recv_sem.at[e], {"mp": (m + 1) % n}
        )

    def send_dp(e, src, dst, cut):
        for i in range(1, nd):
            to = (p + i) % nd
            remote(
                src.at[to] if cut else src, dst.at[p], xsend_sem.at[e], xrecv_sem.at[e], {"dp": to}
            ).start()

    def whole_dp(e, dst):
        part = pl.ds(0, nd - 1)
        return remote(
            dst.at[part], dst.at[part], xsend_sem.at[e], xrecv_sem.at[e], {"dp": (p + 1) % nd}
        )

    outs = []

    def store_out(i, src, dst):
        c = pltpu.make_async_copy(src, dst, out_sem.at[i])
        c.start()
        outs.append(c)

    def added(r):
        total = r[0].astype(F32)
        for i in range(1, nd):
            total += r[i].astype(F32)
        return total

    tokens = x_ref.shape[0]
    blocks = (n, tokens // 128, 128)
    flat = (n, tokens)

    loads[0].wait()
    loads[1].wait()
    s1[...] = dot(w1_ref[...], x_ref[...], 0, 1).astype(BF).reshape(blocks)
    pl.semaphore_wait(barrier, n - 1 + nd - 1)
    send_all(0, s1, r1)
    loads[2].wait()
    loads[3].wait()
    s2[...] = dot(w2_ref[...], g_ref[...], 1, 1).astype(BF).reshape(blocks)
    send_all(1, s2, r2)
    loads[4].wait()
    loads[5].wait()
    ut_ref[...] = u_ref[...].T
    dt_ref[...] = d_ref[...].T
    acc_ref[...] = w1_ref[...].astype(F32).T
    reorder(rel_ref, acc_ref, 0, DEPTH, True)
    w1t_ref[...] = rel_ref[...].astype(BF)

    half = tokens // 2
    whole(0, s1, r1).wait_recv()
    col_ref[...] = r1[...].reshape(flat)
    for q in range(2):
        cols = pl.ds(q * half, half)
        a = dot(ut_ref[...], col_ref[:, cols], 1, 0)
        sq = a * a
        th = jnp.tanh(C0 * (a + C1 * (a * sq)))
        up = 0.5 * (1.0 + th)
        hid = (a * up).astype(BF)
        hid_ref[:, cols] = hid
        slope_ref[:, cols] = a
        th_ref[:, cols] = th
        mid_ref[:, cols] = dot(dt_ref[...], hid, 1, 0).astype(BF)
    s3[...] = mid_ref[...].reshape(blocks)
    send_all(2, s3, r3)

    for q in range(2):
        cols = pl.ds(q * half, half)
        a, th = slope_ref[:, cols], th_ref[:, cols]
        slope_ref[:, cols] = 0.5 * (1.0 + th) + (0.5 * a) * (1.0 - th * th) * (
            C0 + (3.0 * C0 * C1) * (a * a)
        )

    whole(1, s2, r2).wait_recv()
    gcol_ref[...] = r2[...].reshape(flat)
    td[...] = dot(hid_ref[...], gcol_ref[...], 1, 1).astype(BF).reshape(td.shape)
    send_dp(1, td, rd, True)
    for q in range(2):
        cols = pl.ds(q * half, half)
        gh = dot(d_ref[...], gcol_ref[:, cols], 1, 0)
        gp = (gh * slope_ref[:, cols]).astype(BF)
        gp_ref[:, cols] = gp
        mid_ref[:, cols] = dot(u_ref[...], gp, 1, 0).astype(BF)
    s4[...] = mid_ref[...].reshape(blocks)
    for base in bases:
        put_last(base + 2 * slot_z[FAR], FAR, 4)
    r4[(DEPTH - 1) * plane + yc] = s4[m]
    send_last(1, 3)
    tu[...] = dot(col_ref[...], gp_ref[...], 1, 1).astype(BF).reshape(tu.shape)
    send_dp(0, tu, ru, True)
    send_last(3, 9)
    ru[p] = tu[p]
    rd[p] = td[p]
    whole_dp(0, ru).wait()
    au[p] = added(ru).astype(BF)
    whole_dp(1, rd).wait()
    ad[p] = added(rd).astype(BF)
    send_dp(3, au.at[p], au, False)
    send_dp(4, ad.at[p], ad, False)
    send_last(9, FAR + 1)
    send_last(FAR + 1, DEPTH - 1)
    for base in bases[:-1]:
        put_last(base + 2 * z, DEPTH - 1, 4)


    whole(2, s3, r3).wait_recv()
    rows = r3[...].reshape(flat)
    t_oo[...] = dot(rows, g_ref[...], 1, 0).astype(BF)
    send_dp(2, t_oo, r_oo, False)
    r_oo[p] = t_oo[...]
    mixed_v[...] = dot(rows, w2_ref[...], 0, 0).astype(BF)

    store_out(0, mixed_v, mixed_ref)


    early = FAR * plane
    first_part = r4.at[pl.ds(0, early)]
    remote(first_part, first_part, send_sem.at[3], recv_sem.at[3], {"mp": (m + 1) % n}).wait_recv()
    rows = r4[:early].reshape(early, tokens)
    t_oi[...] = dot(rows, x_ref[...], 1, 0).astype(BF)
    send_dp(5, t_oi, r_oi, False)
    r_oi[p] = t_oi[...]

    whole_dp(2, r_oo).wait()
    w2g_v[...] = added(r_oo) * factor
    store_out(5, w2g_v, w2g_ref)
    whole(0, s1, r1).wait_send()
    whole(1, s2, r2).wait_send()
    whole(2, s3, r3).wait_send()
    whole_dp(3, au).wait()
    ug_v[...] = au[...].astype(F32).reshape(ug_ref.shape) * factor
    store_out(3, ug_v, ug_ref)
    whole_dp(4, ad).wait()
    dg_v[...] = ad[...].astype(F32).reshape(dg_ref.shape) * factor
    store_out(4, dg_v, dg_ref)

    last_part = r4.at[pl.ds(early, n - 1 - early)]
    remote(last_part, last_part, send_sem.at[3], recv_sem.at[4], {"mp": (m + 1) % n}).wait_recv()
    rows = r4[early:].reshape(n - early, tokens)
    t_oj[...] = dot(rows, x_ref[...], 1, 0).astype(BF)
    send_dp(6, t_oj, r_oj, False)
    r_oj[p] = t_oj[...]
    igrad_v[...] = dot(r4[...].reshape(flat), w1t_ref[...], 0, 0).astype(BF)
    store_out(1, igrad_v, igrad_ref)
    whole_dp(5, r_oi).wait()
    rel_ref[:early] = added(r_oi) * factor
    reorder(acc_ref, rel_ref, 0, FAR, False)
    whole(3, s4, r4).wait_send()
    whole_dp(6, r_oj).wait()
    rel_ref[early:] = added(r_oj) * factor
    reorder(acc_ref, rel_ref, FAR, DEPTH, False)
    w1g_v[...] = acc_ref[...].T
    store_out(2, w1g_v, w1g_ref)
    for c in outs:
        c.wait()


def store(*refs):
    src, dst, mid, sem = refs[:6], refs[6:12], refs[12:18], refs[18]
    into = [pltpu.make_async_copy(src[i], mid[i], sem.at[i]) for i in range(6)]
    out = [pltpu.make_async_copy(mid[i], dst[i], sem.at[6 + i]) for i in range(6)]
    for c in into:
        c.start()
    for i in range(6):
        into[i].wait()
        out[i].start()
    for c in out:
        c.wait()


def local(n, nd, inputs, out_grad, outer_in, inner_up, inner_down, outer_out):
    t, _, k = inputs.shape
    h = inner_up.shape[2]
    x, g = inputs.reshape(t, k), out_grad.reshape(t, k)
    w1, u, d, w2 = outer_in[0], inner_up[0], inner_down[0], outer_out[0]
    shape = jax.ShapeDtypeStruct
    vm = pltpu.VMEM
    lanes = t // 128
    early = FAR * (n // DEPTH)
    blocks = vm((n, lanes, 128), BF)
    outs = pl.pallas_call(
        functools.partial(kernel, n, nd, float(t * nd) ** -0.5),
        out_shape=(
            shape((t, k), BF),
            shape((t, k), BF),
            shape((k, n), F32),
            shape((n, h), F32),
            shape((h, n), F32),
            shape((n, k), F32),
        ),
        in_specs=[pl.BlockSpec(memory_space=pl.ANY)] * 6,
        out_specs=[pl.BlockSpec(memory_space=pl.ANY)] * 6,
        scratch_shapes=[
            vm((t, k), BF),
            vm((t, k), BF),
            vm((k, n), BF),
            vm((n, h), BF),
            vm((h, n), BF),
            vm((n, k), BF),
            vm((h, n), BF),
            vm((n, h), BF),
            vm((n, k), BF),
            vm((n, k), F32),
            vm((n, k), F32),
        ]
        + [blocks] * 8
        + [
            vm((n, t), BF),
            vm((n, t), BF),
            vm((h, t), F32),
            vm((h, t), F32),
            vm((h, t), BF),
            vm((h, t), BF),
            vm((n, t), BF),
            vm((nd, n // nd, h), BF),
            vm((nd, h // nd, n), BF),
            vm((nd, n // nd, h), BF),
            vm((nd, h // nd, n), BF),
            vm((nd, n // nd, h), BF),
            vm((nd, h // nd, n), BF),
            vm((n, k), BF),
            vm((nd, n, k), BF),
            vm((early, k), BF),
            vm((nd, early, k), BF),
            vm((n - early, k), BF),
            vm((nd, n - early, k), BF),
            pltpu.SemaphoreType.DMA((6,)),
            pltpu.SemaphoreType.DMA((4,)),
            pltpu.SemaphoreType.DMA((5,)),
            pltpu.SemaphoreType.DMA((7,)),
            pltpu.SemaphoreType.DMA((7,)),
            pltpu.SemaphoreType.DMA((6,)),
            vm((t, k), BF),
            vm((t, k), BF),
            vm((k, n), F32),
            vm((n, h), F32),
            vm((h, n), F32),
            vm((n, k), F32),
        ],
        compiler_params=pltpu.CompilerParams(
            collective_id=0, has_side_effects=True, vmem_limit_bytes=62 * 1024 * 1024
        ),
    )(x, g, w1, u, d, w2)
    outs = pl.pallas_call(
        store,
        out_shape=tuple(shape(o.shape, o.dtype) for o in outs),
        in_specs=[pl.BlockSpec(memory_space=pl.ANY)] * 6,
        out_specs=[pl.BlockSpec(memory_space=pl.ANY)] * 6,
        scratch_shapes=[vm(o.shape, o.dtype) for o in outs] + [pltpu.SemaphoreType.DMA((12,))],
        compiler_params=pltpu.CompilerParams(vmem_limit_bytes=62 * 1024 * 1024),
    )(*outs)
    mixed, igrad, w1g, ug, dg, w2g = outs
    return (
        mixed.reshape(t, 1, k),
        igrad.reshape(t, 1, k),
        w1g[None],
        ug[None],
        dg[None],
        w2g[None],
    )


def solution(mesh):
    n, nd = mesh.shape["mp"], mesh.shape["dp"]
    specs = (
        P("dp", "mp", None),
        P("dp", "mp", None),
        P("mp", None, None),
        P("mp", None, None),
        P("mp", None, None),
        P("mp", None, None),
    )
    return jax.shard_map(
        functools.partial(local, n, nd), mesh=mesh, in_specs=specs, out_specs=specs, check_vma=False
    )
```
